32 devices in a mesh: seq: 4 (over y, x), dp: 8 (over z, core).
Axes of the slice: x: 2, y: 2, z: 4, core: 2. Of those that a mesh axis runs over, the one named last changes fastest.
Arguments:
- hidden_in: bfloat16 [16, 1024, 1024], P('dp', 'seq'), may hold values from -6 to 6
- documents: int32 [16, 1024], P('dp'), may hold values from 0 to 2, as said below
- cotangent: bfloat16 [16, 1024, 1024], P('dp', 'seq'), may hold values from -6 to 6
- mixer_gain: bfloat16 [1024], P(('seq', 'dp')), may hold values from 0.5 to 1.5
- mamba_gate: bfloat16 [1024, 1536], P(('seq', 'dp')), may hold values from -0.1875 to 0.1875
- mamba_input: bfloat16 [1024, 1792], P(('seq', 'dp')), may hold values from -0.1875 to 0.1875
- step_weight: bfloat16 [1024, 24], P(('seq', 'dp')), may hold values from -0.1875 to 0.1875
- conv_taps: bfloat16 [4, 1792], P(None, ('seq', 'dp')), may hold values from -3 to 3
- conv_bias: bfloat16 [1792], P(('seq', 'dp')), may hold values from -3 to 3
- step_bias: float32 [24], replicated, may hold values from -7 to -3
- decay_log: float32 [24], replicated, may hold values from -1 to 1.5
- skip_scale: float32 [24], replicated, may hold values from 0.5 to 1.5
- mamba_gain: bfloat16 [1536], P(('seq', 'dp')), may hold values from 0.5 to 1.5
- mamba_output: bfloat16 [1536, 1024], P(('seq', 'dp')), may hold values from -0.15625 to 0.15625
- query_weight: bfloat16 [1024, 512], P(('seq', 'dp')), may hold values from -0.1875 to 0.1875
- keyvalue_matrix: bfloat16 [1024, 256], P(('seq', 'dp')), may hold values from -0.1875 to 0.1875
- attn_output: bfloat16 [512, 1024], P(('seq', 'dp')), may hold values from -3 to 3
- ffn_gain: bfloat16 [1024], P(('seq', 'dp')), may hold values from 0.5 to 1.5
- gate_up: bfloat16 [1024, 4096], P(('seq', 'dp')), may hold values from -0.1875 to 0.1875
- down_weight: bfloat16 [2048, 1024], P(('seq', 'dp')), may hold values from -0.125 to 0.125
Outputs:
- layer_out: bfloat16 [16, 1024, 1024], P('dp', 'seq')
- grad_input: bfloat16 [16, 1024, 1024], P('dp', 'seq')
- grad_mixer_gain: float32 [1024], P(('seq', 'dp'))
- grad_mamba_gate: float32 [1024, 1536], P(('seq', 'dp'))
- grad_mamba_input: float32 [1024, 1792], P(('seq', 'dp'))
- grad_step_weight: float32 [1024, 24], P(('seq', 'dp'))
- grad_conv_taps: float32 [4, 1792], P(None, ('seq', 'dp'))
- grad_conv_bias: float32 [1792], P(('seq', 'dp'))
- grad_step_bias: float32 [24], replicated
- grad_decay_log: float32 [24], replicated
- grad_skip_scale: float32 [24], replicated
- grad_mamba_gain: float32 [1536], P(('seq', 'dp'))
- grad_mamba_output: float32 [1536, 1024], P(('seq', 'dp'))
- grad_query_weight: float32 [1024, 512], P(('seq', 'dp'))
- grad_keyvalue_weight: float32 [1024, 256], P(('seq', 'dp'))
- grad_attn_output: float32 [512, 1024], P(('seq', 'dp'))
- grad_ffn_gain: float32 [1024], P(('seq', 'dp'))
- grad_gate_up: float32 [1024, 4096], P(('seq', 'dp'))
- grad_down_weight: float32 [2048, 1024], P(('seq', 'dp'))
The draws below stay inside these ranges and needn't reach their ends.
Inputs may be any that keep to these rules, and one draw needn't show every extreme that they name: Each row holds documents 0, 1, 2 in order: document 0 has 1 to 128 tokens at the row's start, document 2 has 1 to 128 tokens at its end, document 1 the rest.
All inputs are finite; a program needn't handle non-finite values.
Results may differ from the reference program's by a relative error of at most 0.014.
Values may be sent and summed in bfloat16 or wider, within the bound.
A program may use at most 256 MiB of HBM per device.

```python
import jax
import jax.numpy as jnp
from jax import lax

MODEL_DIM = 1024
FF = 2048
QUERY_HEADS = 8
KEYVALUE_HEADS = 2
HEAD_SIZE = 64
NH = 24
HP = 64
STATE = 128
KW = 4
PIECE = 256
SEQ_DEV = 2
DS = 1536
CD = 1792
LENGTH = 1024
SEQS = 16


def draw_documents(key, part):
    key = jax.random.fold_in(key, 11)
    head_key, tail_key = jax.random.split(key)
    head_len = jax.random.randint(head_key, (SEQS, 1), 1, PIECE // 2 + 1)
    tail_len = jax.random.randint(tail_key, (SEQS, 1), 1, PIECE // 2 + 1)
    places = lax.broadcasted_iota(jnp.int32, (SEQS, LENGTH), 1)
    return (places >= head_len).astype(jnp.int32) + (places >= LENGTH - tail_len).astype(jnp.int32)


def block_levels(own_key, extent, shards, least, high):
    def one(dim, shards_of):
        steps = jax.random.uniform(jax.random.fold_in(jax.random.fold_in(own_key, 6), dim), (shards_of,), jnp.float32, least / len(shards), high / len(shards))
        return jnp.repeat(jnp.exp(steps), extent[dim] // shards_of).reshape((-1,) + (1,) * (len(extent) - dim - 1))

    factor_of = one(*shards[0])
    for cut in shards[1:]:
        factor_of = factor_of * one(*cut)
    return factor_of


def centred(own_key, extent, deviation, limit, shards=(), kind=jnp.bfloat16):
    entries = deviation * jax.random.normal(own_key, extent, jnp.float32)
    if shards:
        entries = entries * block_levels(own_key, extent, shards, -0.22, 0.18)
    return jnp.clip(entries, -limit, limit).astype(kind)


def setup_inputs(seed: int = 0) -> dict:
    seeds = jax.random.split(jax.random.key(seed), 21)
    hidden_in = centred(seeds[0], (SEQS, LENGTH, MODEL_DIM), 1.0, 6.0, ((0, 8), (1, 4)))
    documents = draw_documents(jax.random.fold_in(seeds[20], 71), 0)
    cotangent = centred(seeds[2], (SEQS, LENGTH, MODEL_DIM), 1.0, 6.0, ((0, 8), (1, 4)))
    mixer_gain = jnp.clip(1.0 + 0.1 * jax.random.normal(seeds[3], (MODEL_DIM,), jnp.float32), 0.5, 1.5).astype(jnp.bfloat16)
    mamba_gate = centred(seeds[4], (MODEL_DIM, DS), MODEL_DIM ** -0.5, 0.1875, ((0, 32),))
    mamba_input = centred(seeds[5], (MODEL_DIM, CD), MODEL_DIM ** -0.5, 0.1875, ((0, 32),))
    step_weight = centred(seeds[6], (MODEL_DIM, NH), MODEL_DIM ** -0.5, 0.1875, ((0, 32),))
    conv_taps = centred(seeds[7], (KW, CD), KW ** -0.5, 3.0, ((1, 32),))
    conv_bias = centred(seeds[8], (CD,), 0.5, 3.0, ((0, 32),))
    step_bias = jnp.clip(jax.random.uniform(seeds[9], (NH,), jnp.float32, -7.0, -3.0), -7.0, -3.0)
    decay_log = jnp.clip(jax.random.uniform(seeds[10], (NH,), jnp.float32, -1.0, 1.5), -1.0, 1.5)
    skip_scale = jnp.clip(jax.random.uniform(seeds[11], (NH,), jnp.float32, 0.5, 1.5), 0.5, 1.5)
    mamba_gain = jnp.clip(1.0 + 0.1 * jax.random.normal(seeds[12], (DS,), jnp.float32), 0.5, 1.5).astype(jnp.bfloat16)
    mamba_output = centred(seeds[13], (DS, MODEL_DIM), DS ** -0.5, 0.15625, ((0, 32),))
    query_weight = centred(seeds[14], (MODEL_DIM, QUERY_HEADS * HEAD_SIZE), MODEL_DIM ** -0.5, 0.1875, ((0, 32),))
    keyvalue_matrix = centred(seeds[15], (MODEL_DIM, 2 * KEYVALUE_HEADS * HEAD_SIZE), MODEL_DIM ** -0.5, 0.1875, ((0, 32),))
    attn_output = centred(seeds[16], (QUERY_HEADS * HEAD_SIZE, MODEL_DIM), 4 ** -0.5, 3.0, ((0, 32),))
    ffn_gain = jnp.clip(1.0 + 0.1 * jax.random.normal(seeds[17], (MODEL_DIM,), jnp.float32), 0.5, 1.5).astype(jnp.bfloat16)
    gate_up = centred(seeds[18], (MODEL_DIM, 2 * FF), MODEL_DIM ** -0.5, 0.1875, ((0, 32),))
    down_weight = centred(seeds[19], (FF, MODEL_DIM), FF ** -0.5, 0.125, ((0, 32),))
    return {"hidden_in": hidden_in, "documents": documents, "cotangent": cotangent, "mixer_gain": mixer_gain, "mamba_gate": mamba_gate, "mamba_input": mamba_input, "step_weight": step_weight, "conv_taps": conv_taps, "conv_bias": conv_bias, "step_bias": step_bias, "decay_log": decay_log, "skip_scale": skip_scale, "mamba_gain": mamba_gain, "mamba_output": mamba_output, "query_weight": query_weight, "keyvalue_matrix": keyvalue_matrix, "attn_output": attn_output, "ffn_gain": ffn_gain, "gate_up": gate_up, "down_weight": down_weight}


EPSILON = 1e-05
THETA_BASE = 100000000000.0
TOP_PRECISION = lax.Precision.HIGHEST

@jax.custom_vjp
def low(v):
    return lax.optimization_barrier(v.astype(jnp.bfloat16)).astype(jnp.float32)

@jax.custom_vjp
def lowered_backward(v):
    return v

def low_keep(v):
    return (low(v), None)

def low_pass(kept, grad):
    return (grad,)

def back_keep(v):
    return (v, None)

def back_low(kept, grad):
    return (low(grad),)
low.defvjp(low_keep, low_pass)
lowered_backward.defvjp(back_keep, back_low)

def matmul(left_side, right_side):
    return jnp.dot(left_side, right_side, precision=TOP_PRECISION, preferred_element_type=jnp.float32)

def rms_scale(values):
    return values * lax.rsqrt(lax.optimization_barrier(jnp.mean(values * values, axis=-1, keepdims=True)) + EPSILON)

def rotate(values, places):
    head_view = values.reshape(values.shape[0], -1, HEAD_SIZE)
    half_head = HEAD_SIZE // 2
    frequencies = jnp.exp(-jnp.log(THETA_BASE) * jnp.arange(half_head, dtype=jnp.float32) / half_head)
    angles = places[:, None] * frequencies[None, :]
    cosine = jnp.cos(angles)[:, None, :]
    sine_vals = jnp.sin(angles)[:, None, :]
    first_half = head_view[:, :, :half_head]
    second_half = head_view[:, :, half_head:]
    turned = jnp.concatenate([first_half * cosine - second_half * sine_vals, second_half * cosine + first_half * sine_vals], axis=2)
    return turned.reshape(values.shape)

def conv_apply(padded, doc_padded, doc_seq, taps, bias):
    count_rows = doc_seq.shape[0]
    summed = jnp.zeros((count_rows, padded.shape[1]), jnp.float32) + bias[None, :]
    for tap_index in range(taps.shape[0]):
        window = padded[tap_index:tap_index + count_rows]
        matched = doc_padded[tap_index:tap_index + count_rows] == doc_seq
        summed = summed + jnp.where(matched[:, None], window, 0.0) * taps[tap_index][None, :]
    return summed

def piece_carry(xs_piece, b_piece, step_piece, log_piece, doc_piece, prev_doc):
    cumulative = jnp.cumsum(log_piece, axis=0)
    at_end = (doc_piece == doc_piece[-1])[:, None]
    weights = jnp.where(at_end, jnp.exp(cumulative[-1][None, :] - cumulative), 0.0) * step_piece
    states = jnp.einsum('qh,qhp,qn->hpn', weights, xs_piece, b_piece, precision=TOP_PRECISION)
    decays = jnp.where(doc_piece[-1] == prev_doc, jnp.exp(cumulative[-1]), 0.0)
    return (decays, states)

def piece_output(xs_piece, b_piece, c_piece, step_piece, log_piece, doc_piece, prev_doc, carried, skip_scale):
    cumulative = jnp.cumsum(log_piece, axis=0)
    local_rows = log_piece.shape[0]
    row_index = lax.broadcasted_iota(jnp.int32, (local_rows, local_rows), 0)
    col_index = lax.broadcasted_iota(jnp.int32, (local_rows, local_rows), 1)
    linked = (row_index >= col_index) & (doc_piece[:, None] == doc_piece[None, :])
    spread = cumulative.T[:, :, None] - cumulative.T[:, None, :]
    factors = jnp.where(linked[None], jnp.exp(jnp.where(linked[None], spread, 0.0)), 0.0)
    inner_prod = jnp.dot(c_piece, b_piece.T, precision=TOP_PRECISION, preferred_element_type=jnp.float32)
    mixing = factors * inner_prod[None] * step_piece.T[:, None, :]
    result = jnp.einsum('hts,shp->thp', mixing, xs_piece, precision=TOP_PRECISION)
    entering = jnp.where((doc_piece == prev_doc)[:, None], jnp.exp(cumulative), 0.0)
    from_state = jnp.einsum('tn,hpn->thp', c_piece, carried, precision=TOP_PRECISION)
    return result + entering[:, :, None] * from_state + skip_scale[None, :, None] * xs_piece

def ssm_sequence(xs_seq, b_seq, c_seq, step_seq, log_seq, doc_seq, skip_scale):
    piece_count = xs_seq.shape[0] // PIECE

    def blocked(values):
        return values.reshape((piece_count, PIECE) + values.shape[1:])
    doc_blocks = blocked(doc_seq)
    prev_docs = jnp.concatenate([jnp.full((1,), -1, jnp.int32), doc_blocks[:-1, -1]])

    def advance(carried, block_in):
        xs_b, b_b, c_b, step_b, log_b, doc_b, prev_b = block_in
        output = piece_output(xs_b, b_b, c_b, step_b, log_b, doc_b, prev_b, carried, skip_scale)
        decays, states = piece_carry(xs_b, b_b, step_b, log_b, doc_b, prev_b)
        return (decays[:, None, None] * carried + states, output)
    zero_state = jnp.zeros((NH, HP, STATE), jnp.float32)
    last_state, outputs = lax.scan(jax.checkpoint(advance), zero_state, (blocked(xs_seq), blocked(b_seq), blocked(c_seq), blocked(step_seq), blocked(log_seq), doc_blocks, prev_docs))
    return outputs.reshape(xs_seq.shape)

def attend(query_block, keyvalue_pairs, doc_seq):
    sequence_length = query_block.shape[0]
    key_span_width = KEYVALUE_HEADS * HEAD_SIZE
    query_head_rows = query_block.reshape(sequence_length, KEYVALUE_HEADS, QUERY_HEADS // KEYVALUE_HEADS, HEAD_SIZE)
    key_head_rows = keyvalue_pairs[:, :key_span_width].reshape(sequence_length, KEYVALUE_HEADS, HEAD_SIZE)
    value_head_rows = keyvalue_pairs[:, key_span_width:].reshape(sequence_length, KEYVALUE_HEADS, HEAD_SIZE)
    score_matrix = lowered_backward(jnp.einsum('lbon,ybn->boly', query_head_rows, key_head_rows, precision=TOP_PRECISION) * HEAD_SIZE ** (-0.5))
    places = jnp.arange(sequence_length)
    allowed = (places[:, None] >= places[None, :]) & (doc_seq[:, None] == doc_seq[None, :])
    masked = jnp.where(allowed[None, None], score_matrix, -1e+30)
    row_peak = lax.optimization_barrier(jnp.max(masked, axis=-1, keepdims=True))
    exp_scores = jnp.exp(masked - row_peak)
    softmax_row_block = low(exp_scores / lax.optimization_barrier(jnp.sum(exp_scores, axis=-1, keepdims=True)))
    merged_heads = jnp.einsum('vyka,avo->kvyo', softmax_row_block, value_head_rows, precision=TOP_PRECISION)
    return merged_heads.reshape(sequence_length, QUERY_HEADS * HEAD_SIZE)

def layer_forward(hidden_rows, doc_group, mixer_gain, mamba_gate, mamba_input, step_weight, conv_taps, conv_bias, step_bias, decay_log, skip_scale, mamba_gain, mamba_output, query_weight, keyvalue_matrix, attn_output, ffn_gain, gate_up, down_weight):
    group_count, sequence_length, model_width = hidden_rows.shape
    flat_rows = hidden_rows.reshape(-1, model_width)
    normed = low(rms_scale(flat_rows) * mixer_gain)
    gate_pre = lowered_backward(matmul(normed, mamba_gate))
    conv_in = low(lowered_backward(matmul(normed, mamba_input)))
    step_raw = lowered_backward(matmul(normed, step_weight))
    query_raw = lowered_backward(matmul(normed, query_weight))
    keyvalue_raw = lowered_backward(matmul(normed, keyvalue_matrix))
    places = jnp.tile(jnp.arange(sequence_length, dtype=jnp.float32), group_count)
    key_span_width = KEYVALUE_HEADS * HEAD_SIZE
    query_block = low(rotate(query_raw, places))
    keyvalue_pairs = low(jnp.concatenate([rotate(keyvalue_raw[:, :key_span_width], places), keyvalue_raw[:, key_span_width:]], axis=1))
    conv_width = conv_in.shape[1]
    rim_width = conv_taps.shape[0] - 1
    conv_seq = conv_in.reshape(group_count, sequence_length, conv_width)
    padded = jnp.concatenate([jnp.zeros((group_count, rim_width, conv_width), jnp.float32), conv_seq], axis=1)
    doc_padded = jnp.concatenate([jnp.full((group_count, rim_width), -1, jnp.int32), doc_group], axis=1)
    conv_out = jax.vmap(conv_apply, in_axes=(0, 0, 0, None, None))(padded, doc_padded, doc_group, conv_taps, conv_bias)
    conv_act = low(jax.nn.silu(conv_out))
    xs_all = conv_act[:, :, :DS].reshape(group_count, sequence_length, NH, HP)
    b_all = conv_act[:, :, DS:DS + STATE]
    c_all = conv_act[:, :, DS + STATE:]
    steps_dt = jax.nn.softplus(step_raw + step_bias[None, :])
    log_decay = -steps_dt * jnp.exp(decay_log)[None, :]
    step_seq = steps_dt.reshape(group_count, sequence_length, NH)
    log_seq = log_decay.reshape(group_count, sequence_length, NH)

    def ssm_one(block_in):
        return ssm_sequence(block_in[0], block_in[1], block_in[2], block_in[3], block_in[4], block_in[5], skip_scale)
    ssm_out = lax.map(ssm_one, (xs_all, b_all, c_all, step_seq, log_seq, doc_group))
    gated_rows = ssm_out.reshape(-1, DS) * jax.nn.silu(gate_pre)
    mamba_norm = low(rms_scale(gated_rows) * mamba_gain)
    mamba_branch = lowered_backward(matmul(mamba_norm, mamba_output))

    def attend_one(block_in):
        return attend(block_in[0], block_in[1], block_in[2])
    attn_mix = lax.map(jax.checkpoint(attend_one), (query_block.reshape(group_count, sequence_length, -1), keyvalue_pairs.reshape(group_count, sequence_length, -1), doc_group))
    attn_mix = low(lowered_backward(attn_mix.reshape(-1, QUERY_HEADS * HEAD_SIZE)))
    attn_branch = lowered_backward(matmul(attn_mix, attn_output))
    mixed_rows = flat_rows + mamba_branch + attn_branch
    normed_two = low(rms_scale(mixed_rows) * ffn_gain)
    gate_up_out = lowered_backward(matmul(normed_two, gate_up))
    gate_part = gate_up_out[:, :FF]
    up_part = gate_up_out[:, FF:]
    ffn_act = low(jax.nn.silu(gate_part) * up_part)
    ffn_branch = lowered_backward(matmul(ffn_act, down_weight))
    return (mixed_rows + ffn_branch).reshape(hidden_rows.shape)

def reference(hidden_in, documents, cotangent, mixer_gain, mamba_gate, mamba_input, step_weight, conv_taps, conv_bias, step_bias, decay_log, skip_scale, mamba_gain, mamba_output, query_weight, keyvalue_matrix, attn_output, ffn_gain, gate_up, down_weight):
    weights = tuple((weight_item.astype(jnp.float32) for weight_item in (mixer_gain, mamba_gate, mamba_input, step_weight, conv_taps, conv_bias, step_bias, decay_log, skip_scale, mamba_gain, mamba_output, query_weight, keyvalue_matrix, attn_output, ffn_gain, gate_up, down_weight)))
    block_count = SEQS // SEQ_DEV
    inputs = hidden_in.astype(jnp.float32).reshape(block_count, SEQ_DEV, LENGTH, MODEL_DIM)
    cot_blocks = cotangent.astype(jnp.float32).reshape(block_count, SEQ_DEV, LENGTH, MODEL_DIM)
    doc_blocks = documents.reshape(block_count, SEQ_DEV, LENGTH)

    def group_step(totals, block_in):
        rows_in, cot_in, doc_in = block_in

        def forward(rows_arg, *weight_args):
            return layer_forward(rows_arg, doc_in, *weight_args)
        result, pullback = jax.vjp(forward, rows_in, *weights)
        gradients = pullback(cot_in)
        totals = tuple((running + adding for running, adding in zip(totals, gradients[1:])))
        return (totals, (result.astype(jnp.bfloat16), gradients[0].astype(jnp.bfloat16)))
    totals, (results, input_grads) = lax.scan(group_step, tuple((jnp.zeros_like(weight_item) for weight_item in weights)), (inputs, cot_blocks, doc_blocks))
    return (results.reshape(SEQS, LENGTH, MODEL_DIM), input_grads.reshape(SEQS, LENGTH, MODEL_DIM), totals[0], totals[1], totals[2], totals[3], totals[4], totals[5], totals[6], totals[7], totals[8], totals[9], totals[10], totals[11], totals[12], totals[13], totals[14], totals[15], totals[16])
```

```python
import jax
import jax.numpy as jnp
from jax import lax
from jax.sharding import PartitionSpec as P

QUERY_HEADS = 8
KEYVALUE_HEADS = 2
HEAD_SIZE = 64


EPSILON = 1e-05
THETA_BASE = 100000000000.0
TOP_PRECISION = lax.Precision.DEFAULT
AXES = ("seq", "dp")
LANES = 128


def passed_along(block, axis, distance):
    devices = range(lax.axis_size(axis))
    route = [(i - distance, i) for i in devices if i - distance in devices]
    return lax.ppermute(block, axis, route)


def pieces_of(decays, states):
    seqs, heads, rows, cols = states.shape
    high = decays.astype(jnp.bfloat16)
    low = (decays - high.astype(jnp.float32)).astype(jnp.bfloat16)
    pair = jnp.pad(jnp.stack([high, low], axis=1), ((0, 0), (0, 14), (0, cols - heads)))
    packed = jnp.concatenate(
        [states.astype(jnp.bfloat16).reshape(seqs, heads * rows, cols), pair], axis=1
    )
    everything = lax.all_gather(packed, "seq")
    split = heads * rows
    tail = everything[:, :, split : split + 2, :heads].astype(jnp.float32)
    all_states = everything[:, :, :split].astype(jnp.float32)
    return tail[:, :, 0] + tail[:, :, 1], all_states.reshape(-1, seqs, heads, rows, cols)


def carried_states(decays, states, forward):
    count, mine = (lax.axis_size("seq"), lax.axis_index("seq"))
    all_decays, all_states = pieces_of(decays, states)
    total = jnp.zeros_like(states)
    order = range(count - 1) if forward else range(count - 1, 0, -1)
    for at in order:
        reached = at < mine if forward else at > mine
        longer = all_decays[at][..., None, None] * total + all_states[at]
        total = jnp.where(reached, longer, total)
    return total


def product(left_side, right_side):
    return jnp.dot(left_side, right_side, preferred_element_type=jnp.float32)


def product_tn(left_side, right_side):
    return lax.dot_general(
        left_side, right_side, (((0,), (0,)), ((), ())), preferred_element_type=jnp.float32
    )


def product_nt(left_side, right_side):
    return lax.dot_general(
        left_side, right_side, (((1,), (1,)), ((), ())), preferred_element_type=jnp.float32
    )


def silu_slope(values):
    sigma = jax.nn.sigmoid(values)
    return sigma * (1.0 + values * (1.0 - sigma))


def norm_back(values, inverse, grad_out):
    return inverse * grad_out - values * inverse**3 * jnp.mean(
        grad_out * values, axis=-1, keepdims=True
    )


def rotate(values, places):
    head_view = values.reshape(values.shape[0], -1, HEAD_SIZE)
    half_head = HEAD_SIZE // 2
    frequencies = jnp.exp(
        -jnp.log(THETA_BASE) * jnp.arange(half_head, dtype=jnp.float32) / half_head
    )
    angles = places[:, None] * frequencies[None, :]
    cosine = jnp.cos(angles)[:, None, :]
    sine_vals = jnp.sin(angles)[:, None, :]
    first_half = head_view[:, :, :half_head]
    second_half = head_view[:, :, half_head:]
    turned = jnp.concatenate(
        [
            first_half * cosine - second_half * sine_vals,
            second_half * cosine + first_half * sine_vals,
        ],
        axis=2,
    )
    return turned.reshape(values.shape)


def conv_apply(padded, doc_padded, doc_seq, taps, bias):
    count_rows = doc_seq.shape[0]
    summed = jnp.zeros((count_rows, padded.shape[1]), jnp.float32) + bias[None, :]
    for tap_index in range(taps.shape[0]):
        window = padded[tap_index : tap_index + count_rows]
        matched = doc_padded[tap_index : tap_index + count_rows] == doc_seq
        summed = summed + jnp.where(matched[:, None], window, 0.0) * taps[tap_index][None, :]
    return summed


def piece_carry(xs_piece, b_piece, step_piece, log_piece, doc_piece, prev_doc):
    cumulative = jnp.cumsum(log_piece, axis=0)
    at_end = (doc_piece == doc_piece[-1])[:, None]
    weights = jnp.where(at_end, jnp.exp(cumulative[-1][None, :] - cumulative), 0.0) * step_piece
    states = jnp.einsum("qh,qhp,qn->hpn", weights, xs_piece, b_piece, precision=TOP_PRECISION)
    decays = jnp.where(doc_piece[-1] == prev_doc, jnp.exp(cumulative[-1]), 0.0)
    return (decays, states)


def piece_output(
    xs_piece, b_piece, c_piece, step_piece, log_piece, doc_piece, prev_doc, carried, skip_scale
):
    cumulative = jnp.cumsum(log_piece, axis=0)
    local_rows = log_piece.shape[0]
    row_index = lax.broadcasted_iota(jnp.int32, (local_rows, local_rows), 0)
    col_index = lax.broadcasted_iota(jnp.int32, (local_rows, local_rows), 1)
    linked = (row_index >= col_index) & (doc_piece[:, None] == doc_piece[None, :])
    spread = cumulative.T[:, :, None] - cumulative.T[:, None, :]
    factors = jnp.where(linked[None], jnp.exp(jnp.where(linked[None], spread, 0.0)), 0.0)
    inner_prod = jnp.dot(
        c_piece, b_piece.T, precision=TOP_PRECISION, preferred_element_type=jnp.float32
    )
    mixing = factors * inner_prod[None] * step_piece.T[:, None, :]
    result = jnp.einsum("hts,shp->thp", mixing, xs_piece, precision=TOP_PRECISION)
    entering = jnp.where((doc_piece == prev_doc)[:, None], jnp.exp(cumulative), 0.0)
    from_state = jnp.einsum("tn,hpn->thp", c_piece, carried, precision=TOP_PRECISION)
    return result + entering[:, :, None] * from_state + skip_scale[None, :, None] * xs_piece


def score_block(query_row_block, keyvalue_rows, doc_query, doc_keys, query_places):
    local_rows = query_row_block.shape[0]
    local_keys = keyvalue_rows.shape[0]
    key_span_width = KEYVALUE_HEADS * HEAD_SIZE
    query_head_rows = query_row_block.reshape(
        local_rows, KEYVALUE_HEADS, QUERY_HEADS // KEYVALUE_HEADS, HEAD_SIZE
    )
    key_head_rows = keyvalue_rows[:, :key_span_width].reshape(local_keys, KEYVALUE_HEADS, HEAD_SIZE)
    score_matrix = jnp.einsum(
        "lbon,ybn->boly", query_head_rows, key_head_rows, preferred_element_type=jnp.float32
    ) * HEAD_SIZE ** (-0.5)
    allowed = (query_places[:, None] >= jnp.arange(local_keys)[None, :]) & (
        doc_query[:, None] == doc_keys[None, :]
    )
    return jnp.where(allowed[None, None], score_matrix, -1e30)


def attend_forward(query_row_block, keyvalue_rows, doc_query, doc_keys, query_places):
    local_rows = query_row_block.shape[0]
    local_keys = keyvalue_rows.shape[0]
    key_span_width = KEYVALUE_HEADS * HEAD_SIZE
    masked = score_block(query_row_block, keyvalue_rows, doc_query, doc_keys, query_places)
    row_peak = jnp.max(masked, axis=-1, keepdims=True)
    exp_scores = jnp.exp(masked - row_peak)
    row_total = jnp.sum(exp_scores, axis=-1, keepdims=True)
    softmax_row_block = (exp_scores / row_total).astype(jnp.bfloat16)
    value_head_rows = keyvalue_rows[:, key_span_width:].reshape(
        local_keys, KEYVALUE_HEADS, HEAD_SIZE
    )
    merged_heads = jnp.einsum(
        "vyka,avo->kvyo", softmax_row_block, value_head_rows, preferred_element_type=jnp.float32
    )
    return (
        merged_heads.reshape(local_rows, QUERY_HEADS * HEAD_SIZE),
        row_peak + jnp.log(row_total),
    )


def attend_backward(
    query_row_block, keyvalue_rows, doc_query, doc_keys, query_places, log_norm, mixed_gradient
):
    local_rows = query_row_block.shape[0]
    local_keys = keyvalue_rows.shape[0]
    key_span_width = KEYVALUE_HEADS * HEAD_SIZE
    masked = score_block(query_row_block, keyvalue_rows, doc_query, doc_keys, query_places)
    softmax_row_block = jnp.exp(masked - log_norm)
    query_head_rows = query_row_block.reshape(
        local_rows, KEYVALUE_HEADS, QUERY_HEADS // KEYVALUE_HEADS, HEAD_SIZE
    )
    key_head_rows = keyvalue_rows[:, :key_span_width].reshape(local_keys, KEYVALUE_HEADS, HEAD_SIZE)
    value_head_rows = keyvalue_rows[:, key_span_width:].reshape(
        local_keys, KEYVALUE_HEADS, HEAD_SIZE
    )
    heads_gradient = mixed_gradient.reshape(
        local_rows, KEYVALUE_HEADS, QUERY_HEADS // KEYVALUE_HEADS, HEAD_SIZE
    )
    grad_probs = jnp.einsum(
        "lbon,ybn->boly", heads_gradient, value_head_rows, preferred_element_type=jnp.float32
    )
    centre = jnp.sum(softmax_row_block * grad_probs, axis=-1, keepdims=True)
    scores_gradient = (softmax_row_block * (grad_probs - centre)).astype(jnp.bfloat16)
    grad_query = jnp.einsum(
        "vyka,avo->kvyo", scores_gradient, key_head_rows, preferred_element_type=jnp.float32
    ) * HEAD_SIZE ** (-0.5)
    grad_key = jnp.einsum(
        "ncuy,uncp->ynp", scores_gradient, query_head_rows, preferred_element_type=jnp.float32
    ) * HEAD_SIZE ** (-0.5)
    grad_value = jnp.einsum(
        "ncuy,uncp->ynp",
        softmax_row_block.astype(jnp.bfloat16),
        heads_gradient,
        preferred_element_type=jnp.float32,
    )
    grad_keyval = jnp.concatenate(
        [
            grad_key.reshape(local_keys, key_span_width),
            grad_value.reshape(local_keys, key_span_width),
        ],
        axis=1,
    )
    return (grad_query.reshape(local_rows, QUERY_HEADS * HEAD_SIZE), grad_keyval)


def local(
    hidden_in,
    documents,
    cotangent,
    mixer_gain,
    mamba_gate,
    mamba_input,
    step_weight,
    conv_taps,
    conv_bias,
    step_bias,
    decay_log,
    skip_scale,
    mamba_gain,
    mamba_output,
    query_weight,
    keyvalue_matrix,
    attn_output,
    ffn_gain,
    gate_up,
    down_weight,
):
    seq_count, piece_len, model_width = hidden_in.shape
    seq_rank = lax.axis_index("seq")
    first_row = seq_rank * piece_len
    devices = lax.axis_size(AXES)
    rows_one = mamba_gate.shape[0]
    width_gate, width_input = mamba_gate.shape[1], mamba_input.shape[1]
    width_query, width_keyvalue = query_weight.shape[1], keyvalue_matrix.shape[1]
    width_step = step_weight.shape[1]
    small_parts = [mixer_gain, conv_taps.reshape(-1), conv_bias, mamba_gain, ffn_gain]
    small = jnp.concatenate(small_parts)
    width_small = -(-small.size // rows_one)
    small = jnp.pad(small, (0, width_small * rows_one - small.size)).reshape(rows_one, width_small)
    width_main = width_gate + width_input + width_query + width_keyvalue
    rest = -(width_step + width_small) % LANES
    first_pack = jnp.concatenate(
        [
            mamba_gate,
            mamba_input,
            query_weight,
            keyvalue_matrix,
            step_weight,
            small,
            jnp.zeros((rows_one, rest), small.dtype),
        ],
        axis=1,
    )
    second_pack = jnp.concatenate([mamba_output, attn_output], axis=0)
    first_full = lax.all_gather(first_pack, AXES, axis=0, tiled=True)
    first_full, second_pack, third_pack, fourth_pack = lax.optimization_barrier(
        (first_full, second_pack, gate_up, down_weight)
    )
    second_full = lax.all_gather(second_pack, AXES, axis=0)
    gate_up_full = lax.all_gather(third_pack, AXES, axis=0, tiled=True)
    down_full = lax.all_gather(fourth_pack, AXES, axis=0, tiled=True)
    main_full = first_full[:, :width_main]
    step_full = first_full[:, width_main : width_main + width_step]
    small_full = first_full[:, width_main + width_step : width_main + width_step + width_small]
    small_full = small_full.reshape(devices, -1)
    small_out = []
    spot = 0
    for part in small_parts:
        small_out.append(small_full[:, spot : spot + part.size])
        spot += part.size
    gain_one = small_out[0].reshape(-1)
    taps_full = small_out[1].reshape(devices, conv_taps.shape[0], -1)
    taps_full = taps_full.transpose(1, 0, 2).reshape(conv_taps.shape[0], -1)
    bias_full = small_out[2].reshape(-1)
    gain_mamba = small_out[3].reshape(-1)
    gain_two = small_out[4].reshape(-1)
    rows_output = mamba_output.shape[0]
    output_full = second_full[:, :rows_output].reshape(-1, mamba_output.shape[1])
    attn_full = second_full[:, rows_output:].reshape(-1, attn_output.shape[1])
    rim_width = taps_full.shape[0] - 1
    doc_own = lax.dynamic_slice_in_dim(documents, first_row, piece_len, 1)
    doc_rim = lax.dynamic_slice_in_dim(
        documents, jnp.maximum(first_row - rim_width, 0), rim_width, 1
    )
    doc_rim = jnp.where(seq_rank > 0, doc_rim, -1)
    prev_doc = doc_rim[:, -1]
    flat_rows = hidden_in.reshape(-1, model_width).astype(jnp.float32)
    inv_one = lax.rsqrt(jnp.mean(flat_rows * flat_rows, axis=-1, keepdims=True) + EPSILON)
    gain_first = gain_one.astype(jnp.float32)
    normed = (flat_rows * inv_one * gain_first).astype(jnp.bfloat16)
    main_raw = product(normed, main_full)
    at_query = width_gate + width_input
    gate_pre = main_raw[:, :width_gate]
    conv_in = main_raw[:, width_gate:at_query].astype(jnp.bfloat16)
    step_raw = product(normed, step_full)
    query_raw = main_raw[:, at_query : at_query + width_query]
    keyvalue_raw = main_raw[:, at_query + width_query :]
    conv_width = conv_in.shape[1]
    conv_seq = conv_in.reshape(seq_count, piece_len, conv_width)
    rim_rows = passed_along(conv_seq[:, piece_len - rim_width :, :], "seq", 1)
    padded = jnp.concatenate([rim_rows, conv_seq], axis=1).astype(jnp.float32)
    doc_padded = jnp.concatenate([doc_rim, doc_own], axis=1)

    def conv_fn(pad_in, taps_in, bias_in):
        return jax.vmap(conv_apply, in_axes=(0, 0, 0, None, None))(
            pad_in, doc_padded, doc_own, taps_in, bias_in
        )

    conv_out, conv_pull = jax.vjp(
        conv_fn, padded, taps_full.astype(jnp.float32), bias_full.astype(jnp.float32)
    )
    conv_act = jax.nn.silu(conv_out).astype(jnp.bfloat16)
    ssm_width = gate_pre.shape[1]
    heads_ssm = step_raw.shape[1]
    state_width = (conv_width - ssm_width) // 2
    act_float = conv_act.astype(jnp.float32)
    xs_all = act_float[:, :, :ssm_width].reshape(
        seq_count, piece_len, heads_ssm, ssm_width // heads_ssm
    )
    b_all = act_float[:, :, ssm_width : ssm_width + state_width]
    c_all = act_float[:, :, ssm_width + state_width :]
    step_sum = step_raw + step_bias[None, :]
    steps_dt = jax.nn.softplus(step_sum)
    rates = jnp.exp(decay_log)
    log_decay = -steps_dt * rates[None, :]
    step_seq = steps_dt.reshape(seq_count, piece_len, heads_ssm)
    log_seq = log_decay.reshape(seq_count, piece_len, heads_ssm)

    def carry_fn(xs_in, b_in, step_in, log_in):
        return jax.vmap(piece_carry)(xs_in, b_in, step_in, log_in, doc_own, prev_doc)

    (decays, states), carry_pull = jax.vjp(carry_fn, xs_all, b_all, step_seq, log_seq)
    entered = carried_states(decays, states, True)

    def output_fn(xs_in, b_in, c_in, step_in, log_in, carried_in, skip_in):
        return jax.vmap(piece_output, in_axes=(0, 0, 0, 0, 0, 0, 0, 0, None))(
            xs_in, b_in, c_in, step_in, log_in, doc_own, prev_doc, carried_in, skip_in
        )

    ssm_out, output_pull = jax.vjp(
        output_fn, xs_all, b_all, c_all, step_seq, log_seq, entered, skip_scale
    )
    ssm_flat = ssm_out.reshape(-1, ssm_width)
    gate_act = jax.nn.silu(gate_pre)
    gated_rows = ssm_flat * gate_act
    inv_mamba = lax.rsqrt(jnp.mean(gated_rows * gated_rows, axis=-1, keepdims=True) + EPSILON)
    gain_second_m = gain_mamba.astype(jnp.float32)
    mamba_norm = (gated_rows * inv_mamba * gain_second_m).astype(jnp.bfloat16)
    mamba_branch = product(mamba_norm, output_full)
    query_places = first_row + jnp.arange(piece_len, dtype=jnp.int32)
    places = jnp.tile(query_places.astype(jnp.float32), seq_count)
    key_span_width = keyvalue_raw.shape[1] // 2
    query_block = rotate(query_raw, places).astype(jnp.bfloat16)
    keyvalue_pairs = jnp.concatenate(
        [rotate(keyvalue_raw[:, :key_span_width], places), keyvalue_raw[:, key_span_width:]], axis=1
    ).astype(jnp.bfloat16)
    kv_whole = lax.all_gather(
        keyvalue_pairs.reshape(seq_count, piece_len, 2 * key_span_width), "seq", axis=1, tiled=True
    )
    query_seq = query_block.reshape(seq_count, piece_len, -1)
    attn_mix, log_norm = jax.vmap(attend_forward, in_axes=(0, 0, 0, 0, None))(
        query_seq, kv_whole, doc_own, documents, query_places
    )
    attn_rows = attn_mix.reshape(seq_count * piece_len, -1).astype(jnp.bfloat16)
    attn_branch = product(attn_rows, attn_full)
    mixed_rows = flat_rows + mamba_branch + attn_branch
    inv_two = lax.rsqrt(jnp.mean(mixed_rows * mixed_rows, axis=-1, keepdims=True) + EPSILON)
    gain_second = gain_two.astype(jnp.float32)
    normed_two = (mixed_rows * inv_two * gain_second).astype(jnp.bfloat16)
    gate_up_out = product(normed_two, gate_up_full)
    hidden_units = gate_up_out.shape[1] // 2
    gate_part = gate_up_out[:, :hidden_units]
    up_part = gate_up_out[:, hidden_units:]
    gate_silu = jax.nn.silu(gate_part)
    ffn_act = (gate_silu * up_part).astype(jnp.bfloat16)
    ffn_branch = product(ffn_act, down_full)
    layer_out = (mixed_rows + ffn_branch).astype(jnp.bfloat16).reshape(hidden_in.shape)
    grad_out = cotangent.reshape(-1, model_width).astype(jnp.float32)
    grad_ffn_branch = grad_out.astype(jnp.bfloat16)
    grad_down = product_tn(ffn_act, grad_ffn_branch).astype(jnp.bfloat16)
    grad_act = product_nt(grad_ffn_branch, down_full)
    grad_gate_up_rows = jnp.concatenate(
        [grad_act * up_part * silu_slope(gate_part), grad_act * gate_silu], axis=1
    ).astype(jnp.bfloat16)
    grad_pieces = [
        product_tn(normed_two, grad_gate_up_rows[:, at : at + model_width]).astype(jnp.bfloat16)
        for at in range(0, grad_gate_up_rows.shape[1], model_width)
    ]
    grad_normed_two = product_nt(grad_gate_up_rows, gate_up_full)
    grad_gain_two = jnp.sum(grad_normed_two * mixed_rows * inv_two, axis=0)
    mixed_gradient = grad_out + norm_back(mixed_rows, inv_two, grad_normed_two * gain_second)
    ffn_pack = jnp.concatenate(
        [part.reshape(devices, -1, model_width) for part in (*grad_pieces, grad_down)], axis=1
    )
    ffn_pack, mixed_gradient = lax.optimization_barrier((ffn_pack, mixed_gradient))
    ffn_sums = lax.psum_scatter(ffn_pack, AXES, scatter_dimension=0)
    grad_branch = mixed_gradient.astype(jnp.bfloat16)
    grad_attn_w = product_tn(attn_rows, grad_branch).astype(jnp.bfloat16)
    grad_attn_rows = product_nt(grad_branch, attn_full).astype(jnp.bfloat16)
    grad_mamba_out_w = product_tn(mamba_norm, grad_branch).astype(jnp.bfloat16)
    grad_mamba_norm = product_nt(grad_branch, output_full)
    grad_gain_mamba = jnp.sum(grad_mamba_norm * gated_rows * inv_mamba, axis=0)
    grad_gated = norm_back(gated_rows, inv_mamba, grad_mamba_norm * gain_mamba.astype(jnp.float32))
    grad_ssm = grad_gated * gate_act
    grad_gate_pre = (grad_gated * ssm_flat * silu_slope(gate_pre)).astype(jnp.bfloat16)
    grad_q_seq, grad_kv_whole = jax.vmap(attend_backward, in_axes=(0, 0, 0, 0, None, 0, 0))(
        query_seq,
        kv_whole,
        doc_own,
        documents,
        query_places,
        log_norm,
        grad_attn_rows.reshape(seq_count, piece_len, -1),
    )
    grad_kv_own = lax.psum_scatter(
        grad_kv_whole.astype(jnp.bfloat16), "seq", scatter_dimension=1, tiled=True
    ).astype(jnp.float32)
    grad_query_raw = rotate(grad_q_seq.reshape(seq_count * piece_len, -1), -places).astype(
        jnp.bfloat16
    )
    grad_kv_flat = grad_kv_own.reshape(seq_count * piece_len, 2 * key_span_width)
    grad_keyvalue_raw = jnp.concatenate(
        [rotate(grad_kv_flat[:, :key_span_width], -places), grad_kv_flat[:, key_span_width:]],
        axis=1,
    ).astype(jnp.bfloat16)
    grad_xs_one, grad_b_one, grad_c_one, grad_step_one, grad_log_one, grad_entered, grad_skip = (
        output_pull(grad_ssm.reshape(ssm_out.shape))
    )
    leaving = carried_states(decays, grad_entered, False)
    grad_decays = jnp.sum(leaving * entered, axis=(2, 3))
    grad_xs_two, grad_b_two, grad_step_two, grad_log_two = carry_pull((grad_decays, leaving))
    grad_log = (grad_log_one + grad_log_two).reshape(-1, heads_ssm)
    grad_steps = (grad_step_one + grad_step_two).reshape(-1, heads_ssm) - grad_log * rates[None, :]
    grad_decay_log = jnp.sum(grad_log * log_decay, axis=0)
    grad_step_sum = grad_steps * jax.nn.sigmoid(step_sum)
    grad_step_bias = jnp.sum(grad_step_sum, axis=0)
    grad_step_raw = grad_step_sum.astype(jnp.bfloat16)
    grad_conv_act = jnp.concatenate(
        [
            (grad_xs_one + grad_xs_two).reshape(seq_count, piece_len, ssm_width),
            grad_b_one + grad_b_two,
            grad_c_one,
        ],
        axis=2,
    )
    grad_conv = grad_conv_act * silu_slope(conv_out)
    grad_padded, grad_taps, grad_conv_b = conv_pull(grad_conv)
    rim_grads = passed_along(grad_padded[:, :rim_width, :].astype(jnp.bfloat16), "seq", -1).astype(
        jnp.float32
    )
    grad_conv_in = grad_padded[:, rim_width:, :] + jnp.concatenate(
        [jnp.zeros((seq_count, piece_len - rim_width, conv_width), jnp.float32), rim_grads], axis=1
    )
    grad_conv_in = grad_conv_in.reshape(-1, conv_width).astype(jnp.bfloat16)
    grad_main = jnp.concatenate(
        [grad_gate_pre, grad_conv_in, grad_query_raw, grad_keyvalue_raw], axis=1
    )
    grad_normed = product_nt(grad_main, main_full) + product_nt(grad_step_raw, step_full)
    main_pieces = [
        product_tn(normed, grad_main[:, at : at + model_width]).astype(jnp.bfloat16)
        for at in range(0, width_main, model_width)
    ]
    grad_step_w = product_tn(normed, grad_step_raw).astype(jnp.bfloat16)
    grad_gain_one = jnp.sum(grad_normed * flat_rows * inv_one, axis=0)
    grad_input = (
        (mixed_gradient + norm_back(flat_rows, inv_one, grad_normed * gain_first))
        .astype(jnp.bfloat16)
        .reshape(hidden_in.shape)
    )
    taps_count = conv_taps.shape[0]
    grad_taps = grad_taps.reshape(taps_count, devices, -1).transpose(1, 0, 2)
    small_grads = jnp.concatenate(
        [
            part.reshape(devices, -1)
            for part in (grad_gain_one, grad_taps, grad_conv_b, grad_gain_mamba, grad_gain_two)
        ],
        axis=1,
    ).astype(jnp.bfloat16)
    small_rows = [
        jnp.pad(part, ((0, 0), (0, model_width - part.shape[1])))[:, None, :]
        for part in (grad_step_w.reshape(devices, -1), small_grads)
    ]
    mixer_parts = [
        part.reshape(devices, -1, model_width)
        for part in (*main_pieces, grad_mamba_out_w, grad_attn_w)
    ]
    spare = jnp.zeros((devices, 14, model_width), jnp.bfloat16)
    mixer_pack = jnp.concatenate([*mixer_parts, *small_rows, spare], axis=1)
    head_grads = jnp.stack([grad_step_bias, grad_decay_log, grad_skip])
    head_sums = jnp.sum(lax.all_gather(head_grads, AXES), axis=0)
    grad_step_bias, grad_decay_log, grad_skip = head_sums[0], head_sums[1], head_sums[2]
    mixer_pack, ffn_sums = lax.optimization_barrier((mixer_pack, ffn_sums))
    mixer_sums = lax.psum_scatter(mixer_pack, AXES, scatter_dimension=0).astype(jnp.float32)
    ffn_sums = ffn_sums.astype(jnp.float32)

    def widened(rows, count):
        return jnp.concatenate([rows[i * rows_one : (i + 1) * rows_one] for i in range(count)], 1)

    ffn_count = len(grad_pieces)
    grad_gate_up_w = widened(ffn_sums, ffn_count)
    grad_down = ffn_sums[ffn_count * rows_one :]
    main_count = len(main_pieces)
    main_sums = widened(mixer_sums, main_count)
    grad_gate_w = main_sums[:, :width_gate]
    grad_input_w = main_sums[:, width_gate:at_query]
    grad_query_w = main_sums[:, at_query : at_query + width_query]
    grad_keyvalue_w = main_sums[:, at_query + width_query :]
    at_row = main_count * rows_one
    grad_mamba_out_w = mixer_sums[at_row : at_row + rows_output]
    at_row += rows_output
    grad_attn_w = mixer_sums[at_row : at_row + attn_output.shape[0]]
    at_row += attn_output.shape[0]
    grad_step_w = mixer_sums[at_row, : step_weight.size].reshape(step_weight.shape)
    small_out = []
    spot = 0
    for part in small_parts:
        small_out.append(mixer_sums[at_row + 1, spot : spot + part.size])
        spot += part.size
    grad_gain_one = small_out[0]
    grad_taps = small_out[1].reshape(taps_count, -1)
    grad_conv_b = small_out[2]
    grad_gain_mamba = small_out[3]
    grad_gain_two = small_out[4]
    return (
        layer_out,
        grad_input,
        grad_gain_one,
        grad_gate_w,
        grad_input_w,
        grad_step_w,
        grad_taps,
        grad_conv_b,
        grad_step_bias,
        grad_decay_log,
        grad_skip,
        grad_gain_mamba,
        grad_mamba_out_w,
        grad_query_w,
        grad_keyvalue_w,
        grad_attn_w,
        grad_gain_two,
        grad_gate_up_w,
        grad_down,
    )


def solution(mesh):
    in_specs = (
        P("dp", "seq", None),
        P("dp", None),
        P("dp", "seq", None),
        P(("seq", "dp")),
        P(("seq", "dp"), None),
        P(("seq", "dp"), None),
        P(("seq", "dp"), None),
        P(None, ("seq", "dp")),
        P(("seq", "dp")),
        P(),
        P(),
        P(),
        P(("seq", "dp")),
        P(("seq", "dp"), None),
        P(("seq", "dp"), None),
        P(("seq", "dp"), None),
        P(("seq", "dp"), None),
        P(("seq", "dp")),
        P(("seq", "dp"), None),
        P(("seq", "dp"), None),
    )
    out_specs = (
        P("dp", "seq", None),
        P("dp", "seq", None),
        P(("seq", "dp")),
        P(("seq", "dp"), None),
        P(("seq", "dp"), None),
        P(("seq", "dp"), None),
        P(None, ("seq", "dp")),
        P(("seq", "dp")),
        P(),
        P(),
        P(),
        P(("seq", "dp")),
        P(("seq", "dp"), None),
        P(("seq", "dp"), None),
        P(("seq", "dp"), None),
        P(("seq", "dp"), None),
        P(("seq", "dp")),
        P(("seq", "dp"), None),
        P(("seq", "dp"), None),
    )
    return jax.shard_map(local, mesh=mesh, in_specs=in_specs, out_specs=out_specs, check_vma=False)
```

```python
import jax
import jax.numpy as jnp
from jax import lax
from jax.sharding import PartitionSpec as P

QUERY_HEADS = 8
KEYVALUE_HEADS = 2
HEAD_SIZE = 64


EPSILON = 1e-05
THETA_BASE = 100000000000.0
TOP_PRECISION = lax.Precision.DEFAULT
AXES = ("seq", "dp")
LANES = 128


def passed_along(block, axis, distance):
    if lax.axis_size(axis) == 1:
        return jnp.zeros_like(block)
    devices = range(lax.axis_size(axis))
    route = [(i - distance, i) for i in devices if i - distance in devices]
    return lax.ppermute(block, axis, route)


def carried_states(decays, states, direction):
    seqs, heads, rows, cols = states.shape
    high = decays.astype(jnp.bfloat16)
    low = (decays - high.astype(jnp.float32)).astype(jnp.bfloat16)
    pair = jnp.pad(jnp.stack([high, low], axis=1), ((0, 0), (0, 14), (0, cols - heads)))
    split = heads * rows
    packed = jnp.concatenate(
        [states.astype(jnp.bfloat16).reshape(seqs, split, cols), pair], axis=1
    )
    total, passed = 0.0, 1.0
    for distance in range(1, lax.axis_size("seq")):
        arrived = passed_along(packed, "seq", direction * distance).astype(jnp.float32)
        tail = arrived[:, split] + arrived[:, split + 1]
        far_states = arrived[:, :split].reshape(states.shape)
        total = total + passed * far_states
        passed = passed * tail[:, :heads, None, None]
    return total


def product(left_side, right_side):
    return jnp.dot(left_side, right_side, preferred_element_type=jnp.float32)


def product_tn(left_side, right_side):
    return lax.dot_general(
        left_side, right_side, (((0,), (0,)), ((), ())), preferred_element_type=jnp.float32
    )


def product_nt(left_side, right_side):
    return lax.dot_general(
        left_side, right_side, (((1,), (1,)), ((), ())), preferred_element_type=jnp.float32
    )


def silu_slope(values):
    sigma = jax.nn.sigmoid(values)
    return sigma * (1.0 + values * (1.0 - sigma))


def norm_back(values, inverse, grad_out):
    return inverse * grad_out - values * inverse**3 * jnp.mean(
        grad_out * values, axis=-1, keepdims=True
    )


def rotate(values, places):
    head_view = values.reshape(values.shape[0], -1, HEAD_SIZE)
    half_head = HEAD_SIZE // 2
    frequencies = jnp.exp(
        -jnp.log(THETA_BASE) * jnp.arange(half_head, dtype=jnp.float32) / half_head
    )
    angles = places[:, None] * frequencies[None, :]
    cosine = jnp.cos(angles)[:, None, :]
    sine_vals = jnp.sin(angles)[:, None, :]
    first_half = head_view[:, :, :half_head]
    second_half = head_view[:, :, half_head:]
    turned = jnp.concatenate(
        [
            first_half * cosine - second_half * sine_vals,
            second_half * cosine + first_half * sine_vals,
        ],
        axis=2,
    )
    return turned.reshape(values.shape)


def conv_apply(padded, doc_padded, doc_seq, taps, bias):
    count_rows = doc_seq.shape[0]
    summed = jnp.zeros((count_rows, padded.shape[1]), jnp.float32) + bias[None, :]
    for tap_index in range(taps.shape[0]):
        window = padded[tap_index : tap_index + count_rows]
        matched = doc_padded[tap_index : tap_index + count_rows] == doc_seq
        summed = summed + jnp.where(matched[:, None], window, 0.0) * taps[tap_index][None, :]
    return summed


def running_sum(log_seq):
    rows = log_seq.shape[1]
    lower = jnp.tril(jnp.ones((rows, rows), jnp.float32))
    return jnp.einsum("ts,bsh->bth", lower, log_seq, precision=lax.Precision.HIGHEST)


def piece_carry(xs_piece, b_piece, step_piece, cumulative, doc_piece, prev_doc):
    at_end = (doc_piece == doc_piece[-1])[:, None]
    weights = jnp.where(at_end, jnp.exp(cumulative[-1][None, :] - cumulative), 0.0) * step_piece
    states = jnp.einsum("qh,qhp,qn->hpn", weights, xs_piece, b_piece, precision=TOP_PRECISION)
    decays = jnp.where(doc_piece[-1] == prev_doc, jnp.exp(cumulative[-1]), 0.0)
    return (decays, states)


def piece_output(
    xs_piece, b_piece, c_piece, step_piece, cumulative, doc_piece, prev_doc, carried, skip_scale
):
    local_rows = cumulative.shape[0]
    row_index = lax.broadcasted_iota(jnp.int32, (local_rows, local_rows), 0)
    col_index = lax.broadcasted_iota(jnp.int32, (local_rows, local_rows), 1)
    linked = (row_index >= col_index) & (doc_piece[:, None] == doc_piece[None, :])
    spread = cumulative.T[:, :, None] - cumulative.T[:, None, :]
    factors = jnp.where(linked[None], jnp.exp(jnp.where(linked[None], spread, 0.0)), 0.0)
    inner_prod = jnp.dot(
        c_piece, b_piece.T, precision=TOP_PRECISION, preferred_element_type=jnp.float32
    )
    mixing = factors * inner_prod[None] * step_piece.T[:, None, :]
    result = jnp.einsum("hts,shp->thp", mixing, xs_piece, precision=TOP_PRECISION)
    entering = jnp.where((doc_piece == prev_doc)[:, None], jnp.exp(cumulative), 0.0)
    from_state = jnp.einsum("tn,hpn->thp", c_piece, carried, precision=TOP_PRECISION)
    return result + entering[:, :, None] * from_state + skip_scale[None, :, None] * xs_piece


def score_block(query_row_block, keyvalue_rows, doc_query, doc_keys, query_places, key_places):
    local_rows = query_row_block.shape[0]
    local_keys = keyvalue_rows.shape[0]
    key_span_width = KEYVALUE_HEADS * HEAD_SIZE
    query_head_rows = query_row_block.reshape(
        local_rows, KEYVALUE_HEADS, QUERY_HEADS // KEYVALUE_HEADS, HEAD_SIZE
    )
    key_head_rows = keyvalue_rows[:, :key_span_width].reshape(local_keys, KEYVALUE_HEADS, HEAD_SIZE)
    score_matrix = jnp.einsum(
        "lbon,ybn->boly", query_head_rows, key_head_rows, preferred_element_type=jnp.float32
    ) * HEAD_SIZE ** (-0.5)
    allowed = (query_places[:, None] >= key_places[None, :]) & (
        doc_query[:, None] == doc_keys[None, :]
    )
    return jnp.where(allowed[None, None], score_matrix, -1e30)


def attend_forward(query_row_block, keyvalue_rows, doc_query, doc_keys, query_places, key_places):
    local_rows = query_row_block.shape[0]
    local_keys = keyvalue_rows.shape[0]
    key_span_width = KEYVALUE_HEADS * HEAD_SIZE
    masked = score_block(query_row_block, keyvalue_rows, doc_query, doc_keys, query_places, key_places)
    row_peak = jnp.max(masked, axis=-1, keepdims=True)
    exp_scores = jnp.exp(masked - row_peak)
    row_total = jnp.sum(exp_scores, axis=-1, keepdims=True)
    softmax_row_block = (exp_scores / row_total).astype(jnp.bfloat16)
    value_head_rows = keyvalue_rows[:, key_span_width:].reshape(
        local_keys, KEYVALUE_HEADS, HEAD_SIZE
    )
    merged_heads = jnp.einsum(
        "vyka,avo->kvyo", softmax_row_block, value_head_rows, preferred_element_type=jnp.float32
    )
    return (
        merged_heads.reshape(local_rows, QUERY_HEADS * HEAD_SIZE),
        row_peak + jnp.log(row_total),
    )


def attend_backward(
    query_row_block, keyvalue_rows, doc_query, doc_keys, query_places, key_places, log_norm, mixed_gradient
):
    local_rows = query_row_block.shape[0]
    local_keys = keyvalue_rows.shape[0]
    key_span_width = KEYVALUE_HEADS * HEAD_SIZE
    masked = score_block(query_row_block, keyvalue_rows, doc_query, doc_keys, query_places, key_places)
    softmax_row_block = jnp.exp(masked - log_norm)
    query_head_rows = query_row_block.reshape(
        local_rows, KEYVALUE_HEADS, QUERY_HEADS // KEYVALUE_HEADS, HEAD_SIZE
    )
    key_head_rows = keyvalue_rows[:, :key_span_width].reshape(local_keys, KEYVALUE_HEADS, HEAD_SIZE)
    value_head_rows = keyvalue_rows[:, key_span_width:].reshape(
        local_keys, KEYVALUE_HEADS, HEAD_SIZE
    )
    heads_gradient = mixed_gradient.reshape(
        local_rows, KEYVALUE_HEADS, QUERY_HEADS // KEYVALUE_HEADS, HEAD_SIZE
    )
    grad_probs = jnp.einsum(
        "lbon,ybn->boly", heads_gradient, value_head_rows, preferred_element_type=jnp.float32
    )
    centre = jnp.sum(softmax_row_block * grad_probs, axis=-1, keepdims=True)
    scores_gradient = (softmax_row_block * (grad_probs - centre)).astype(jnp.bfloat16)
    grad_query = jnp.einsum(
        "vyka,avo->kvyo", scores_gradient, key_head_rows, preferred_element_type=jnp.float32
    ) * HEAD_SIZE ** (-0.5)
    grad_key = jnp.einsum(
        "ncuy,uncp->ynp", scores_gradient, query_head_rows, preferred_element_type=jnp.float32
    ) * HEAD_SIZE ** (-0.5)
    grad_value = jnp.einsum(
        "ncuy,uncp->ynp",
        softmax_row_block.astype(jnp.bfloat16),
        heads_gradient,
        preferred_element_type=jnp.float32,
    )
    grad_keyval = jnp.concatenate(
        [
            grad_key.reshape(local_keys, key_span_width),
            grad_value.reshape(local_keys, key_span_width),
        ],
        axis=1,
    )
    return (grad_query.reshape(local_rows, QUERY_HEADS * HEAD_SIZE), grad_keyval)


def local(
    hidden_in,
    documents,
    cotangent,
    mixer_gain,
    mamba_gate,
    mamba_input,
    step_weight,
    conv_taps,
    conv_bias,
    step_bias,
    decay_log,
    skip_scale,
    mamba_gain,
    mamba_output,
    query_weight,
    keyvalue_matrix,
    attn_output,
    ffn_gain,
    gate_up,
    down_weight,
):
    seq_count, piece_len, model_width = hidden_in.shape
    seq_rank = lax.axis_index("seq")
    first_row = seq_rank * piece_len
    devices = lax.axis_size(AXES)
    rows_one = mamba_gate.shape[0]
    width_gate, width_input = mamba_gate.shape[1], mamba_input.shape[1]
    width_query, width_keyvalue = query_weight.shape[1], keyvalue_matrix.shape[1]
    width_step = step_weight.shape[1]
    small_parts = [mixer_gain, conv_taps.reshape(-1), conv_bias, mamba_gain, ffn_gain]
    small = jnp.concatenate(small_parts)
    width_small = -(-small.size // rows_one)
    small = jnp.pad(small, (0, width_small * rows_one - small.size)).reshape(rows_one, width_small)
    width_main = width_gate + width_input + width_query + width_keyvalue
    rest = -(width_step + width_small) % LANES
    first_pack = jnp.concatenate(
        [
            mamba_gate,
            mamba_input,
            query_weight,
            keyvalue_matrix,
            step_weight,
            small,
            jnp.zeros((rows_one, rest), small.dtype),
        ],
        axis=1,
    )
    second_pack = jnp.concatenate([mamba_output, attn_output], axis=0)
    first_full = lax.all_gather(first_pack, AXES, axis=0, tiled=True)
    first_full, second_pack, third_pack, fourth_pack = lax.optimization_barrier(
        (first_full, second_pack, gate_up, down_weight)
    )
    second_full = lax.all_gather(second_pack, AXES, axis=0)
    gate_up_full = lax.all_gather(third_pack, AXES, axis=0, tiled=True)
    down_full = lax.all_gather(fourth_pack, AXES, axis=0, tiled=True)
    main_full = first_full[:, :width_main]
    step_full = first_full[:, width_main : width_main + width_step]
    small_full = first_full[:, width_main + width_step : width_main + width_step + width_small]
    small_full = small_full.reshape(devices, -1)
    small_out = []
    spot = 0
    for part in small_parts:
        small_out.append(small_full[:, spot : spot + part.size])
        spot += part.size
    gain_one = small_out[0].reshape(-1)
    taps_full = small_out[1].reshape(devices, conv_taps.shape[0], -1)
    taps_full = taps_full.transpose(1, 0, 2).reshape(conv_taps.shape[0], -1)
    bias_full = small_out[2].reshape(-1)
    gain_mamba = small_out[3].reshape(-1)
    gain_two = small_out[4].reshape(-1)
    rows_output = mamba_output.shape[0]
    output_full = second_full[:, :rows_output].reshape(-1, mamba_output.shape[1])
    attn_full = second_full[:, rows_output:].reshape(-1, attn_output.shape[1])
    rim_width = taps_full.shape[0] - 1
    doc_own = lax.dynamic_slice_in_dim(documents, first_row, piece_len, 1)
    doc_rim = lax.dynamic_slice_in_dim(
        documents, jnp.maximum(first_row - rim_width, 0), rim_width, 1
    )
    doc_rim = jnp.where(seq_rank > 0, doc_rim, -1)
    prev_doc = doc_rim[:, -1]
    flat_rows = hidden_in.reshape(-1, model_width).astype(jnp.float32)
    inv_one = lax.rsqrt(jnp.mean(flat_rows * flat_rows, axis=-1, keepdims=True) + EPSILON)
    gain_first = gain_one.astype(jnp.float32)
    normed = (flat_rows * inv_one * gain_first).astype(jnp.bfloat16)

    def pieces(grads):
        return [
            product_tn(normed, grads[:, at : at + model_width]).astype(jnp.bfloat16)
            for at in range(0, grads.shape[1], model_width)
        ]

    main_raw = product(normed, main_full)
    at_query = width_gate + width_input
    gate_pre = main_raw[:, :width_gate]
    conv_in = main_raw[:, width_gate:at_query].astype(jnp.bfloat16)
    step_raw = product(normed, step_full)
    query_raw = main_raw[:, at_query : at_query + width_query]
    keyvalue_raw = main_raw[:, at_query + width_query :]
    conv_width = conv_in.shape[1]
    conv_seq = conv_in.reshape(seq_count, piece_len, conv_width)
    rim_rows = passed_along(conv_seq[:, piece_len - rim_width :, :], "seq", 1)
    padded = jnp.concatenate([rim_rows, conv_seq], axis=1).astype(jnp.float32)
    doc_padded = jnp.concatenate([doc_rim, doc_own], axis=1)

    def conv_fn(pad_in, taps_in, bias_in):
        return jax.vmap(conv_apply, in_axes=(0, 0, 0, None, None))(
            pad_in, doc_padded, doc_own, taps_in, bias_in
        )

    conv_out, conv_pull = jax.vjp(
        conv_fn, padded, taps_full.astype(jnp.float32), bias_full.astype(jnp.float32)
    )
    conv_act = jax.nn.silu(conv_out).astype(jnp.bfloat16)
    ssm_width = gate_pre.shape[1]
    heads_ssm = step_raw.shape[1]
    state_width = (conv_width - ssm_width) // 2
    act_float = conv_act.astype(jnp.float32)
    xs_all = act_float[:, :, :ssm_width].reshape(
        seq_count, piece_len, heads_ssm, ssm_width // heads_ssm
    )
    b_all = act_float[:, :, ssm_width : ssm_width + state_width]
    c_all = act_float[:, :, ssm_width + state_width :]
    step_sum = step_raw + step_bias[None, :]
    steps_dt = jax.nn.softplus(step_sum)
    rates = jnp.exp(decay_log)
    log_decay = -steps_dt * rates[None, :]
    step_seq = steps_dt.reshape(seq_count, piece_len, heads_ssm)
    log_seq = log_decay.reshape(seq_count, piece_len, heads_ssm)
    sums_seq, sums_pull = jax.vjp(running_sum, log_seq)

    def carry_fn(xs_in, b_in, step_in, log_in):
        return jax.vmap(piece_carry)(xs_in, b_in, step_in, log_in, doc_own, prev_doc)

    (decays, states), carry_pull = jax.vjp(carry_fn, xs_all, b_all, step_seq, sums_seq)
    entered = carried_states(decays, states, 1)

    def output_fn(xs_in, b_in, c_in, step_in, log_in, carried_in, skip_in):
        return jax.vmap(piece_output, in_axes=(0, 0, 0, 0, 0, 0, 0, 0, None))(
            xs_in, b_in, c_in, step_in, log_in, doc_own, prev_doc, carried_in, skip_in
        )

    ssm_out, output_pull = jax.vjp(
        output_fn, xs_all, b_all, c_all, step_seq, sums_seq, entered, skip_scale
    )
    ssm_flat = ssm_out.reshape(-1, ssm_width)
    gate_act = jax.nn.silu(gate_pre)
    gated_rows = ssm_flat * gate_act
    inv_mamba = lax.rsqrt(jnp.mean(gated_rows * gated_rows, axis=-1, keepdims=True) + EPSILON)
    gain_second_m = gain_mamba.astype(jnp.float32)
    mamba_norm = (gated_rows * inv_mamba * gain_second_m).astype(jnp.bfloat16)
    mamba_branch = product(mamba_norm, output_full)
    query_places = first_row + jnp.arange(piece_len, dtype=jnp.int32)
    places = jnp.tile(query_places.astype(jnp.float32), seq_count)
    key_span_width = keyvalue_raw.shape[1] // 2
    query_block = rotate(query_raw, places).astype(jnp.bfloat16)
    keyvalue_pairs = jnp.concatenate(
        [rotate(keyvalue_raw[:, :key_span_width], places), keyvalue_raw[:, key_span_width:]], axis=1
    ).astype(jnp.bfloat16)
    kv_own = keyvalue_pairs.reshape(seq_count, piece_len, 2 * key_span_width)
    seq_peers = lax.axis_size("seq")
    kv_whole = jnp.concatenate(
        [passed_along(kv_own, "seq", far) for far in range(seq_peers - 1, 0, -1)] + [kv_own],
        axis=1,
    )
    before = (seq_peers - 1) * piece_len
    key_places = first_row - before + jnp.arange(seq_peers * piece_len, dtype=jnp.int32)
    doc_keys = lax.dynamic_slice_in_dim(
        jnp.pad(documents, ((0, 0), (before, 0)), constant_values=-1),
        first_row,
        seq_peers * piece_len,
        1,
    )
    query_seq = query_block.reshape(seq_count, piece_len, -1)
    attn_mix, log_norm = jax.vmap(attend_forward, in_axes=(0, 0, 0, 0, None, None))(
        query_seq, kv_whole, doc_own, doc_keys, query_places, key_places
    )
    attn_rows = attn_mix.reshape(seq_count * piece_len, -1).astype(jnp.bfloat16)
    attn_branch = product(attn_rows, attn_full)
    mixed_rows = flat_rows + mamba_branch + attn_branch
    inv_two = lax.rsqrt(jnp.mean(mixed_rows * mixed_rows, axis=-1, keepdims=True) + EPSILON)
    gain_second = gain_two.astype(jnp.float32)
    normed_two = (mixed_rows * inv_two * gain_second).astype(jnp.bfloat16)
    gate_up_out = product(normed_two, gate_up_full)
    hidden_units = gate_up_out.shape[1] // 2
    gate_part = gate_up_out[:, :hidden_units]
    up_part = gate_up_out[:, hidden_units:]
    gate_silu = jax.nn.silu(gate_part)
    ffn_act = (gate_silu * up_part).astype(jnp.bfloat16)
    ffn_branch = product(ffn_act, down_full)
    layer_out = (mixed_rows + ffn_branch).astype(jnp.bfloat16).reshape(hidden_in.shape)
    grad_out = cotangent.reshape(-1, model_width).astype(jnp.float32)
    grad_ffn_branch = grad_out.astype(jnp.bfloat16)
    grad_down = product_tn(ffn_act, grad_ffn_branch).astype(jnp.bfloat16)
    grad_act = product_nt(grad_ffn_branch, down_full)
    grad_gate_up_rows = jnp.concatenate(
        [grad_act * up_part * silu_slope(gate_part), grad_act * gate_silu], axis=1
    ).astype(jnp.bfloat16)
    grad_pieces = [
        product_tn(normed_two, grad_gate_up_rows[:, at : at + model_width]).astype(jnp.bfloat16)
        for at in range(0, grad_gate_up_rows.shape[1], model_width)
    ]
    grad_normed_two = product_nt(grad_gate_up_rows, gate_up_full)
    grad_gain_two = jnp.sum(grad_normed_two * mixed_rows * inv_two, axis=0)
    mixed_gradient = grad_out + norm_back(mixed_rows, inv_two, grad_normed_two * gain_second)
    grad_branch = mixed_gradient.astype(jnp.bfloat16)
    grad_attn_w = product_tn(attn_rows, grad_branch).astype(jnp.bfloat16)
    grad_attn_rows = product_nt(grad_branch, attn_full).astype(jnp.bfloat16)
    grad_mamba_out_w = product_tn(mamba_norm, grad_branch).astype(jnp.bfloat16)
    grad_mamba_norm = product_nt(grad_branch, output_full)
    grad_gain_mamba = jnp.sum(grad_mamba_norm * gated_rows * inv_mamba, axis=0)
    grad_gated = norm_back(gated_rows, inv_mamba, grad_mamba_norm * gain_mamba.astype(jnp.float32))
    grad_ssm = grad_gated * gate_act
    grad_gate_pre = (grad_gated * ssm_flat * silu_slope(gate_pre)).astype(jnp.bfloat16)
    gate_pieces = pieces(grad_gate_pre)
    early_parts = [*grad_pieces, *gate_pieces, grad_down, grad_mamba_out_w, grad_attn_w]
    early_pack = jnp.concatenate(
        [part.reshape(devices, -1, model_width) for part in early_parts], axis=1
    )
    early_pack, grad_attn_rows, grad_ssm = lax.optimization_barrier(
        (early_pack, grad_attn_rows, grad_ssm)
    )
    early_sums = lax.psum_scatter(early_pack, AXES, scatter_dimension=0)
    grad_q_seq, grad_kv_whole = jax.vmap(attend_backward, in_axes=(0, 0, 0, 0, None, None, 0, 0))(
        query_seq,
        kv_whole,
        doc_own,
        doc_keys,
        query_places,
        key_places,
        log_norm,
        grad_attn_rows.reshape(seq_count, piece_len, -1),
    )
    grad_kv_own = grad_kv_whole[:, before:]
    for far in range(1, seq_peers):
        at = before - far * piece_len
        sent = grad_kv_whole[:, at : at + piece_len].astype(jnp.bfloat16)
        grad_kv_own = grad_kv_own + passed_along(sent, "seq", -far).astype(jnp.float32)
    grad_query_raw = rotate(grad_q_seq.reshape(seq_count * piece_len, -1), -places).astype(
        jnp.bfloat16
    )
    grad_kv_flat = grad_kv_own.reshape(seq_count * piece_len, 2 * key_span_width)
    grad_keyvalue_raw = jnp.concatenate(
        [rotate(grad_kv_flat[:, :key_span_width], -places), grad_kv_flat[:, key_span_width:]],
        axis=1,
    ).astype(jnp.bfloat16)
    grad_xs_one, grad_b_one, grad_c_one, grad_step_one, grad_log_one, grad_entered, grad_skip = (
        output_pull(grad_ssm.reshape(ssm_out.shape))
    )
    leaving = carried_states(decays, grad_entered, -1)
    grad_decays = jnp.sum(leaving * entered, axis=(2, 3))
    grad_xs_two, grad_b_two, grad_step_two, grad_log_two = carry_pull((grad_decays, leaving))
    grad_log = sums_pull(grad_log_one + grad_log_two)[0].reshape(-1, heads_ssm)
    grad_steps = (grad_step_one + grad_step_two).reshape(-1, heads_ssm) - grad_log * rates[None, :]
    grad_decay_log = jnp.sum(grad_log * log_decay, axis=0)
    grad_step_sum = grad_steps * jax.nn.sigmoid(step_sum)
    grad_step_bias = jnp.sum(grad_step_sum, axis=0)
    grad_step_raw = grad_step_sum.astype(jnp.bfloat16)
    grad_conv_act = jnp.concatenate(
        [
            (grad_xs_one + grad_xs_two).reshape(seq_count, piece_len, ssm_width),
            grad_b_one + grad_b_two,
            grad_c_one,
        ],
        axis=2,
    )
    grad_conv = grad_conv_act * silu_slope(conv_out)
    grad_padded, grad_taps, grad_conv_b = conv_pull(grad_conv)
    rim_grads = passed_along(grad_padded[:, :rim_width, :].astype(jnp.bfloat16), "seq", -1).astype(
        jnp.float32
    )
    grad_conv_in = grad_padded[:, rim_width:, :] + jnp.concatenate(
        [jnp.zeros((seq_count, piece_len - rim_width, conv_width), jnp.float32), rim_grads], axis=1
    )
    grad_conv_in = grad_conv_in.reshape(-1, conv_width).astype(jnp.bfloat16)
    grad_main = jnp.concatenate(
        [grad_gate_pre, grad_conv_in, grad_query_raw, grad_keyvalue_raw], axis=1
    )
    grad_normed = product_nt(grad_main, main_full) + product_nt(grad_step_raw, step_full)
    late_rows = grad_main[:, width_gate:]
    main_pieces = pieces(late_rows)
    grad_step_w = product_tn(normed, grad_step_raw).astype(jnp.bfloat16)
    grad_gain_one = jnp.sum(grad_normed * flat_rows * inv_one, axis=0)
    grad_input = (
        (mixed_gradient + norm_back(flat_rows, inv_one, grad_normed * gain_first))
        .astype(jnp.bfloat16)
        .reshape(hidden_in.shape)
    )
    taps_count = conv_taps.shape[0]
    grad_taps = grad_taps.reshape(taps_count, devices, -1).transpose(1, 0, 2)
    small_grads = jnp.concatenate(
        [
            part.reshape(devices, -1)
            for part in (grad_gain_one, grad_taps, grad_conv_b, grad_gain_mamba, grad_gain_two)
        ],
        axis=1,
    ).astype(jnp.bfloat16)
    small_rows = [
        jnp.pad(part, ((0, 0), (0, model_width - part.shape[1])))[:, None, :]
        for part in (grad_step_w.reshape(devices, -1), small_grads)
    ]
    mixer_parts = [part.reshape(devices, -1, model_width) for part in main_pieces]
    spare = jnp.zeros((devices, 14, model_width), jnp.bfloat16)
    mixer_pack = jnp.concatenate([*mixer_parts, *small_rows, spare], axis=1)
    head_grads = jnp.stack([grad_step_bias, grad_decay_log, grad_skip])
    head_sums = jnp.sum(lax.all_gather(head_grads, AXES), axis=0)
    grad_step_bias, grad_decay_log, grad_skip = head_sums[0], head_sums[1], head_sums[2]
    mixer_pack, early_sums = lax.optimization_barrier((mixer_pack, early_sums))
    mixer_sums = lax.psum_scatter(mixer_pack, AXES, scatter_dimension=0).astype(jnp.float32)
    early_sums = early_sums.astype(jnp.float32)

    def widened(rows, at, width):
        parts = []
        for spot in range(0, width, model_width):
            wide = min(model_width, width - spot)
            count = rows_one * wide // model_width
            parts.append(rows[at : at + count].reshape(rows_one, wide))
            at += count
        return jnp.concatenate(parts, axis=1), at

    grad_gate_up_w, at_row = widened(early_sums, 0, gate_up.shape[1])
    grad_gate_w, at_row = widened(early_sums, at_row, width_gate)
    grad_down = early_sums[at_row : at_row + down_weight.shape[0]]
    at_row += down_weight.shape[0]
    grad_mamba_out_w = early_sums[at_row : at_row + rows_output]
    at_row += rows_output
    grad_attn_w = early_sums[at_row : at_row + attn_output.shape[0]]
    late_sums, at_row = widened(mixer_sums, 0, width_main - width_gate)
    grad_input_w = late_sums[:, :width_input]
    grad_query_w = late_sums[:, width_input : width_input + width_query]
    grad_keyvalue_w = late_sums[:, width_input + width_query :]
    grad_step_w = mixer_sums[at_row, : step_weight.size].reshape(step_weight.shape)
    small_out = []
    spot = 0
    for part in small_parts:
        small_out.append(mixer_sums[at_row + 1, spot : spot + part.size])
        spot += part.size
    grad_gain_one = small_out[0]
    grad_taps = small_out[1].reshape(taps_count, -1)
    grad_conv_b = small_out[2]
    grad_gain_mamba = small_out[3]
    grad_gain_two = small_out[4]
    return (
        layer_out,
        grad_input,
        grad_gain_one,
        grad_gate_w,
        grad_input_w,
        grad_step_w,
        grad_taps,
        grad_conv_b,
        grad_step_bias,
        grad_decay_log,
        grad_skip,
        grad_gain_mamba,
        grad_mamba_out_w,
        grad_query_w,
        grad_keyvalue_w,
        grad_attn_w,
        grad_gain_two,
        grad_gate_up_w,
        grad_down,
    )


def solution(mesh):
    in_specs = (
        P("dp", "seq", None),
        P("dp", None),
        P("dp", "seq", None),
        P(("seq", "dp")),
        P(("seq", "dp"), None),
        P(("seq", "dp"), None),
        P(("seq", "dp"), None),
        P(None, ("seq", "dp")),
        P(("seq", "dp")),
        P(),
        P(),
        P(),
        P(("seq", "dp")),
        P(("seq", "dp"), None),
        P(("seq", "dp"), None),
        P(("seq", "dp"), None),
        P(("seq", "dp"), None),
        P(("seq", "dp")),
        P(("seq", "dp"), None),
        P(("seq", "dp"), None),
    )
    out_specs = (
        P("dp", "seq", None),
        P("dp", "seq", None),
        P(("seq", "dp")),
        P(("seq", "dp"), None),
        P(("seq", "dp"), None),
        P(("seq", "dp"), None),
        P(None, ("seq", "dp")),
        P(("seq", "dp")),
        P(),
        P(),
        P(),
        P(("seq", "dp")),
        P(("seq", "dp"), None),
        P(("seq", "dp"), None),
        P(("seq", "dp"), None),
        P(("seq", "dp"), None),
        P(("seq", "dp")),
        P(("seq", "dp"), None),
        P(("seq", "dp"), None),
    )
    return jax.shard_map(local, mesh=mesh, in_specs=in_specs, out_specs=out_specs, check_vma=False)
```
